32 devices in a mesh: grp: 2 (over y), subj: 4 (over x, core), vert: 4 (over z).
Axes of the slice: x: 2, y: 2, z: 4, core: 2. Of those that a mesh axis runs over, the one named last changes fastest.
Arguments:
- dosage: bfloat16 [16384, 512], P(('grp', 'subj')), parts along dimension 0, may hold values from 0 to 2
- phenotype: bfloat16 [16384, 20480], P(('grp', 'subj'), 'vert'), parts along dimension 0, may hold values from -12 to 12
- covariates: float32 [16384, 40], P(('grp', 'subj')), parts along dimension 0, may hold values from -7 to 7
Outputs:
- tstat: float32 [1024, 20480], P(('grp', 'subj'), 'vert'), parts along dimension 0
The draws below stay inside these ranges and needn't reach their ends.
There are 2 independent parts, one for each index of `grp`. The reference program is written for one: setup_inputs(seed, part) draws one part's arguments, and reference() takes and returns one part's arrays. A program takes and returns all parts, laid end to end along the dimension named above; each array names one. Nothing has to cross between parts.
All inputs are finite; a program needn't handle non-finite values.
Results may differ from the reference program's by a relative error of at most 0.004.
Values sent between devices are 32-bit elements; how exact they have to be, the bound alone decides.
A program may use at most 192 MiB of HBM per device.

```python
import jax
import jax.numpy as jnp
from jax import lax

COVS = 40
VERTS = 20480
SNPS = 512
SUBJECTS = 8192


def covariate_table(key):
    base = jax.random.fold_in(key, 101)
    key_vals, key_scale, key_centre = jax.random.split(base, 3)
    scale = jnp.exp(jax.random.uniform(key_scale, (COVS,), jnp.float32, jnp.log(0.5), jnp.log(2.0)))
    centre = jax.random.uniform(key_centre, (COVS,), jnp.float32, -1.0, 1.0)
    raw = jnp.clip(jax.random.normal(key_vals, (SUBJECTS, COVS), jnp.float32), -3.0, 3.0)
    return raw * scale[None, :] + centre[None, :]


def draw_covariates(key, part):
    return covariate_table(key)


def draw_phenotype(key, part):
    table = covariate_table(key)
    key_effect, key_noise = jax.random.split(jax.random.fold_in(key, 202), 2)
    effect = jax.random.normal(key_effect, (COVS, VERTS), jnp.float32) * (0.8 / COVS ** 0.5)
    noise = jax.random.normal(key_noise, (SUBJECTS, VERTS), jnp.float32)
    fitted = jnp.dot(table, effect, precision=lax.Precision.HIGHEST)
    return jnp.clip(fitted + noise, -12.0, 12.0).astype(jnp.bfloat16)


def draw_dosage(key, part):
    table = covariate_table(key)
    key_load, key_base, key_noise = jax.random.split(jax.random.fold_in(key, 303), 3)
    column = jnp.arange(COVS)
    strong = column < max(COVS // 4, 1)
    spread = jnp.where(strong, 0.4, 0.05).astype(jnp.float32)
    loading = jax.random.normal(key_load, (COVS, SNPS), jnp.float32) * spread[:, None]
    offset = jax.random.uniform(key_base, (SNPS,), jnp.float32, -2.5, 1.0)
    noise = jax.random.normal(key_noise, (SUBJECTS, SNPS), jnp.float32)
    logit = offset[None, :] + jnp.dot(table, loading, precision=lax.Precision.HIGHEST) + noise
    return (2.0 * jax.nn.sigmoid(logit)).astype(jnp.bfloat16)


def setup_inputs(seed: int = 0, part: int = 0) -> dict:
    key_list = jax.random.split(jax.random.key(seed), 4)
    part_splits = jax.random.split(jax.random.fold_in(key_list[3], part), 4)
    return {
        "dosage": draw_dosage(jax.random.fold_in(jax.random.fold_in(key_list[3], part), 71), part),
        "phenotype": draw_phenotype(jax.random.fold_in(jax.random.fold_in(key_list[3], part), 71), part),
        "covariates": draw_covariates(jax.random.fold_in(jax.random.fold_in(key_list[3], part), 71), part),
    }


def reference(dosage, phenotype, covariates):
    count = covariates.shape[0]
    design = jnp.concatenate([jnp.ones((count, 1), jnp.float32), covariates], axis=1)
    hi = lax.Precision.HIGHEST
    geno = dosage.astype(jnp.float32)
    pheno = phenotype.astype(jnp.float32)
    gram = jnp.dot(design.T, design, precision=hi)
    factor = jnp.linalg.cholesky(gram)
    geno_coef = jax.scipy.linalg.cho_solve((factor, True), jnp.dot(design.T, geno, precision=hi))
    pheno_coef = jax.scipy.linalg.cho_solve((factor, True), jnp.dot(design.T, pheno, precision=hi))
    geno_res = geno - jnp.dot(design, geno_coef, precision=hi)
    pheno_res = pheno - jnp.dot(design, pheno_coef, precision=hi)
    geno_var = lax.optimization_barrier(jnp.sum(geno_res * geno_res, axis=0))
    pheno_var = lax.optimization_barrier(jnp.sum(pheno_res * pheno_res, axis=0))
    cross = jnp.dot(geno_res.astype(jnp.bfloat16).T.astype(jnp.float32), pheno_res.astype(jnp.bfloat16).astype(jnp.float32), preferred_element_type=jnp.float32)
    dof = jnp.float32(count - covariates.shape[1] - 2)
    return cross * jnp.sqrt(dof) / jnp.sqrt(geno_var[:, None] * pheno_var[None, :] - cross * cross)
```

```python
import functools

import jax
import jax.numpy as jnp
from jax import lax
from jax.experimental import pallas as pl
from jax.experimental.pallas import tpu as pltpu
from jax.sharding import PartitionSpec as P

MESH = pl.DeviceIdType.MESH
CORES = 2
HI = lax.Precision.HIGHEST
LAST = (((1,), (1,)), ((), ()))


def split_parts(values):
    upper = values.astype(jnp.bfloat16)
    restored = lax.optimization_barrier(upper).astype(jnp.float32)
    lower = (values - restored).astype(jnp.bfloat16)
    return (upper, lower)


def exchange_kernel(chips, own, kp, tile, xt_ref, p_hbm, cross_ref, b_ref, s_ref,
                    pbuf, yall, recvc, sendx, recvx, bown, brecv, sloc, srecvc, srecvx,
                    psem, csend, crecv, xsend, xrecv, bsend, brcv, scs, scr, sxs, sxr):
    half = chips * own
    kh = kp // 2
    full = 2 * half + kp
    tiles = yall.shape[0]
    s = lax.axis_index("subj")
    core = lax.rem(s, CORES)
    chip = s // CORES
    other = {"subj": chip * CORES + (1 - core)}

    def partner(d):
        return lax.rem(chip + d, chips)

    def peer(d):
        return {"subj": partner(d) * CORES + core}

    def p_copy(i):
        slot = lax.rem(i, 2)
        cols = pl.ds(pl.multiple_of(i * tile, tile), tile)
        return pltpu.make_async_copy(p_hbm.at[:, cols], pbuf.at[slot], psem.at[slot])

    def core_copy(i):
        rows = pl.ds(pl.multiple_of((1 - core) * half, 8), half + kp)
        return pltpu.make_async_remote_copy(
            src_ref=yall.at[i, rows], dst_ref=recvc.at[i], send_sem=csend.at[i],
            recv_sem=crecv.at[i], device_id=other, device_id_type=MESH)

    def x_copy(i, d):
        return pltpu.make_async_remote_copy(
            src_ref=sendx.at[d - 1, i], dst_ref=recvx.at[d - 1, i], send_sem=xsend.at[d - 1, i],
            recv_sem=xrecv.at[d - 1, i], device_id=peer(d), device_id_type=MESH)

    def b_copy(i):
        return pltpu.make_async_remote_copy(
            src_ref=bown.at[i], dst_ref=brecv.at[i], send_sem=bsend.at[i],
            recv_sem=brcv.at[i], device_id=other, device_id_type=MESH)

    def s_core_copy():
        return pltpu.make_async_remote_copy(
            src_ref=sloc.at[0], dst_ref=srecvc, send_sem=scs,
            recv_sem=scr, device_id=other, device_id_type=MESH)

    def s_x_copy(d):
        return pltpu.make_async_remote_copy(
            src_ref=sloc.at[1], dst_ref=srecvx.at[d - 1], send_sem=sxs.at[d - 1],
            recv_sem=sxr.at[d - 1], device_id=peer(d), device_id_type=MESH)

    p_copy(0).start()
    barrier = pltpu.get_barrier_semaphore()
    pl.semaphore_signal(barrier, inc=1, device_id=other, device_id_type=MESH)
    for d in range(1, chips):
        pl.semaphore_signal(barrier, inc=1, device_id=peer(d), device_id_type=MESH)

    dd = jnp.concatenate([xt_ref[half:half + kp, :], xt_ref[full:full + kp, :]], axis=0)
    row = lax.broadcasted_iota(jnp.int32, (kp, half), 0)
    for side in range(2):
        lo = side * (half + kp)
        gx = xt_ref[lo:lo + half, :]
        prod = lax.dot_general(dd, gx, LAST, preferred_element_type=jnp.float32)
        prod = prod[:kp] + prod[kp:]
        sq = jnp.zeros((half, 128), jnp.float32)
        for c in range(gx.shape[1] // 128):
            part = gx[:, c * 128:(c + 1) * 128].astype(jnp.float32)
            sq = sq + part * part
        sq = jnp.sum(sq.T, axis=0, keepdims=True)
        sloc[0, :, side * half:(side + 1) * half] = jnp.where(row == kp - 1, sq, prod)
    gram = lax.dot_general(dd, dd, LAST, preferred_element_type=jnp.float32)
    sloc[0, :, 2 * half:] = jnp.zeros((kp, sloc.shape[2] - 2 * half), jnp.float32)
    sloc[0, :, 2 * half:2 * half + 2 * kp] = gram[:kp] + gram[kp:]
    pl.semaphore_wait(barrier, chips)
    s_core_copy().start()

    own_rows = pl.multiple_of(core * (half + kp) + chip * own, 8)
    shift = pl.multiple_of(core * half, 8)
    b_rows = pl.multiple_of(half + core * kh, 8)

    def produce(i, carry):
        @pl.when(i < tiles)
        def _():
            @pl.when(i + 1 < tiles)
            def _():
                p_copy(i + 1).start()

            p_copy(i).wait()
            p = pbuf[lax.rem(i, 2)]
            y = jnp.dot(xt_ref[...], p, preferred_element_type=jnp.float32)
            pf = p.astype(jnp.float32)
            sq = jnp.sum(pf * pf, axis=0, keepdims=True)
            b = y[half:half + kp] + y[full:full + kp]
            rows = lax.broadcasted_iota(jnp.int32, (kp, tile), 0)
            yall[i, 0:half] = y[0:half]
            yall[i, half:half + kp] = jnp.where(rows == kp - 1, sq, b)
            yall[i, half + kp:full] = y[half + kp:full]
            core_copy(i).start()

        @pl.when(i == 0)
        def _():
            s_core_copy().wait_recv()
            sloc[1] = sloc[0] + srecvc[...]
            for d in range(1, chips):
                s_x_copy(d).start()

        @pl.when(i > 0)
        def _():
            j = i - 1
            core_copy(j).wait_recv()
            bh = yall[j, pl.ds(b_rows, kh)] + recvc[j, pl.ds(pl.multiple_of(b_rows - shift, 8), kh)]
            bown[j] = bh
            for d in range(1, chips):
                r = pl.multiple_of(core * (half + kp) + partner(d) * own, 8)
                sendx[d - 1, j, 0:own] = (
                    yall[j, pl.ds(r, own)] + recvc[j, pl.ds(pl.multiple_of(r - shift, 8), own)])
                sendx[d - 1, j, own:own + kh] = bh
                x_copy(j, d).start()
            cols = pl.ds(pl.multiple_of(j * tile, tile), tile)
            cross_ref[:, cols] = (
                yall[j, pl.ds(own_rows, own)]
                + recvc[j, pl.ds(pl.multiple_of(own_rows - shift, 8), own)])

        return carry

    lax.fori_loop(0, tiles + 1, produce, 0)

    total = sloc[1]
    for d in range(1, chips):
        s_x_copy(d).wait_recv()
        total = total + srecvx[d - 1]
    s_ref[...] = total

    def collect(i, carry):
        @pl.when(i < tiles)
        def _():
            cols = pl.ds(pl.multiple_of(i * tile, tile), tile)
            for d in range(1, chips):
                x_copy(i, d).wait_recv()
                bown[i] = bown[i] + recvx[d - 1, i, own:own + kh]
                cross_ref[:, cols] = cross_ref[:, cols] + recvx[d - 1, i, 0:own]
            b_copy(i).start()

        @pl.when(i > 0)
        def _():
            j = i - 1
            cols = pl.ds(pl.multiple_of(j * tile, tile), tile)
            b_copy(j).wait_recv()
            b_ref[pl.ds(pl.multiple_of(core * kh, 8), kh), cols] = bown[j]
            b_ref[pl.ds(pl.multiple_of((1 - core) * kh, 8), kh), cols] = brecv[j]

        return carry

    lax.fori_loop(0, tiles + 1, collect, 0)

    def drain(i, carry):
        core_copy(i).wait_send()
        b_copy(i).wait_send()
        for d in range(1, chips):
            x_copy(i, d).wait_send()
        return carry

    lax.fori_loop(0, tiles, drain, 0)
    s_core_copy().wait_send()
    for d in range(1, chips):
        s_x_copy(d).wait_send()


def per_device(dosage, phenotype, covariates):
    rows, snps = dosage.shape
    verts = phenotype.shape[1]
    k = covariates.shape[1] + 1
    parts = lax.axis_size("subj")
    chips = parts // CORES
    own = snps // parts
    half = chips * own
    kp = -(-(k + 1) // 16) * 16
    kh = kp // 2
    tile = next(t for t in (512, 256, 128) if verts % t == 0)
    tiles = verts // tile
    wide = 2 * half + -(-2 * kp // 128) * 128

    design = jnp.concatenate([jnp.ones((rows, 1), jnp.float32), covariates], axis=1).T
    upper, lower = split_parts(design)
    pad = ((0, kp - k), (0, 0))
    geno = dosage.T.reshape(chips, CORES, own, rows)
    xt = jnp.concatenate(
        [geno[:, 0].reshape(half, rows), jnp.pad(upper, pad),
         geno[:, 1].reshape(half, rows), jnp.pad(lower, pad)], axis=0)

    f32 = jnp.float32
    vmem = pl.BlockSpec(memory_space=pltpu.VMEM)
    dma = pltpu.SemaphoreType.DMA
    others = chips - 1
    cross, b, s = pl.pallas_call(
        functools.partial(exchange_kernel, chips, own, kp, tile),
        out_shape=[
            jax.ShapeDtypeStruct((own, verts), f32),
            jax.ShapeDtypeStruct((kp, verts), f32),
            jax.ShapeDtypeStruct((kp, wide), f32),
        ],
        in_specs=[vmem, pl.BlockSpec(memory_space=pl.ANY)],
        out_specs=[vmem, vmem, vmem],
        scratch_shapes=[
            pltpu.VMEM((2, rows, tile), jnp.bfloat16),
            pltpu.VMEM((tiles, 2 * half + kp, tile), f32),
            pltpu.VMEM((tiles, half + kp, tile), f32),
            pltpu.VMEM((others, tiles, own + kh, tile), f32),
            pltpu.VMEM((others, tiles, own + kh, tile), f32),
            pltpu.VMEM((tiles, kh, tile), f32),
            pltpu.VMEM((tiles, kh, tile), f32),
            pltpu.VMEM((2, kp, wide), f32),
            pltpu.VMEM((kp, wide), f32),
            pltpu.VMEM((others, kp, wide), f32),
            dma((2,)),
            dma((tiles,)), dma((tiles,)),
            dma((others, tiles)), dma((others, tiles)),
            dma((tiles,)), dma((tiles,)),
            dma, dma,
            dma((others,)), dma((others,)),
        ],
        compiler_params=pltpu.CompilerParams(
            collective_id=0, has_side_effects=True, vmem_limit_bytes=56 * 1024 * 1024
        ),
        cost_estimate=pl.CostEstimate(
            flops=2 * rows * verts * (2 * half + 2 * kp),
            bytes_accessed=2 * rows * verts + 8 * own * verts, transcendentals=0),
    )(xt, phenotype)

    gram = s[:k, 2 * half:2 * half + k] + s[:k, 2 * half + kp:2 * half + kp + k]
    index = lax.axis_index("subj")
    start = lax.rem(index, CORES) * half + (index // CORES) * own
    mine = lax.dynamic_slice_in_dim(s, start, own, 1)
    factor = jnp.linalg.cholesky(gram)
    inverse = jax.scipy.linalg.solve_triangular(factor, jnp.eye(k, dtype=f32), lower=True)
    u = jnp.dot(inverse, mine[:k], precision=HI)
    v = jnp.dot(inverse, b[:k], precision=HI)
    geno_var = mine[kp - 1] - jnp.sum(u * u, axis=0)
    pheno_var = b[kp - 1] - jnp.sum(v * v, axis=0)
    cross = cross - lax.dot_general(u, v, (((0,), (0,)), ((), ())), precision=HI)
    dof = f32(rows * parts - covariates.shape[1] - 2)
    return cross * jnp.sqrt(dof) / jnp.sqrt(geno_var[:, None] * pheno_var[None, :] - cross * cross)


def solution(mesh):
    in_specs = (P(("grp", "subj"), None), P(("grp", "subj"), "vert"), P(("grp", "subj"), None))
    out_specs = P(("grp", "subj"), "vert")
    return jax.shard_map(
        per_device, mesh=mesh, in_specs=in_specs, out_specs=out_specs, check_vma=False
    )
```

```python
import functools

import jax
import jax.numpy as jnp
from jax import lax
from jax.experimental import pallas as pl
from jax.experimental.pallas import tpu as pltpu
from jax.sharding import PartitionSpec as P

MESH = pl.DeviceIdType.MESH
CORES = 2
HI = lax.Precision.HIGHEST
LAST = (((1,), (1,)), ((), ()))


def exchange_kernel(chips, own, k, kp, tile, dof, g_ref, cov_ref, p_hbm, cross_ref,
                    xt_ref, dpad, uts, gvs, btmp, pbuf, yall, recvc, sendx, recvx, bown, brecv, sloc, srecvc, srecvx,
                    psem, csend, crecv, xsend, xrecv, bsend, brcv, scs, scr, sxs, sxr):
    half = chips * own
    kh = kp // 2
    full = 2 * half + kp
    tiles = yall.shape[0]
    s = lax.axis_index("subj")
    core = lax.rem(s, CORES)
    chip = s // CORES
    other = {"subj": chip * CORES + (1 - core)}

    def partner(d):
        return lax.rem(chip + d, chips)

    def peer(d):
        return {"subj": partner(d) * CORES + core}

    def p_copy(i):
        slot = lax.rem(i, 2)
        cols = pl.ds(pl.multiple_of(i * tile, tile), tile)
        return pltpu.make_async_copy(p_hbm.at[:, cols], pbuf.at[slot], psem.at[slot])

    def core_copy(i):
        rows = pl.ds(pl.multiple_of((1 - core) * half, 8), half + kp)
        return pltpu.make_async_remote_copy(
            src_ref=yall.at[i, rows], dst_ref=recvc.at[i], send_sem=csend.at[i],
            recv_sem=crecv.at[i], device_id=other, device_id_type=MESH)

    def x_copy(i, d):
        return pltpu.make_async_remote_copy(
            src_ref=sendx.at[d - 1, i], dst_ref=recvx.at[d - 1, i], send_sem=xsend.at[d - 1, i],
            recv_sem=xrecv.at[d - 1, i], device_id=peer(d), device_id_type=MESH)

    def b_copy(i):
        return pltpu.make_async_remote_copy(
            src_ref=bown.at[i], dst_ref=brecv.at[i], send_sem=bsend.at[i],
            recv_sem=brcv.at[i], device_id=other, device_id_type=MESH)

    def s_core_copy():
        return pltpu.make_async_remote_copy(
            src_ref=sloc.at[0], dst_ref=srecvc, send_sem=scs,
            recv_sem=scr, device_id=other, device_id_type=MESH)

    def s_x_copy(d):
        return pltpu.make_async_remote_copy(
            src_ref=sloc.at[1], dst_ref=srecvx.at[d - 1], send_sem=sxs.at[d - 1],
            recv_sem=sxr.at[d - 1], device_id=peer(d), device_id_type=MESH)

    p_copy(0).start()
    barrier = pltpu.get_barrier_semaphore()
    pl.semaphore_signal(barrier, inc=1, device_id=other, device_id_type=MESH)
    for d in range(1, chips):
        pl.semaphore_signal(barrier, inc=1, device_id=peer(d), device_id_type=MESH)

    lane = lax.broadcasted_iota(jnp.int32, dpad.shape, 1)
    dpad[...] = jnp.where(lane == k - 1, 1.0, 0.0)
    dpad[:, 0:k - 1] = cov_ref[...]
    step = 256
    for r in range(0, g_ref.shape[0], step):
        gt = g_ref[r:r + step, :].T
        for x in range(chips):
            for c in range(CORES):
                to, at = c * (half + kp) + x * own, (x * CORES + c) * own
                xt_ref[to:to + own, r:r + step] = gt[at:at + own]
        dt = dpad[r:r + step, :].T[:kp]
        upper = dt.astype(jnp.bfloat16)
        xt_ref[half:half + kp, r:r + step] = upper
        xt_ref[full:full + kp, r:r + step] = (dt - upper.astype(jnp.float32)).astype(jnp.bfloat16)

    dd = jnp.concatenate([xt_ref[half:half + kp, :], xt_ref[full:full + kp, :]], axis=0)
    row = lax.broadcasted_iota(jnp.int32, (kp, half), 0)
    for side in range(2):
        lo = side * (half + kp)
        gx = xt_ref[lo:lo + half, :]
        prod = lax.dot_general(dd, gx, LAST, preferred_element_type=jnp.float32)
        prod = prod[:kp] + prod[kp:]
        sq = jnp.zeros((half, 128), jnp.float32)
        for c in range(gx.shape[1] // 128):
            part = gx[:, c * 128:(c + 1) * 128].astype(jnp.float32)
            sq = sq + part * part
        sq = jnp.sum(sq.T, axis=0, keepdims=True)
        sloc[0, :, side * half:(side + 1) * half] = jnp.where(row == kp - 1, sq, prod)
    gram = lax.dot_general(dd, dd, LAST, preferred_element_type=jnp.float32)
    sloc[0, :, 2 * half:] = jnp.zeros((kp, sloc.shape[2] - 2 * half), jnp.float32)
    sloc[0, :, 2 * half:2 * half + 2 * kp] = gram[:kp] + gram[kp:]
    pl.semaphore_wait(barrier, chips)
    s_core_copy().start()

    own_rows = pl.multiple_of(core * (half + kp) + chip * own, 8)
    shift = pl.multiple_of(core * half, 8)
    b_rows = pl.multiple_of(half + core * kh, 8)

    def produce(i, carry):
        @pl.when(i < tiles)
        def _():
            @pl.when(i + 1 < tiles)
            def _():
                p_copy(i + 1).start()

            p_copy(i).wait()
            p = pbuf[lax.rem(i, 2)]
            y = jnp.dot(xt_ref[...], p, preferred_element_type=jnp.float32)
            pf = p.astype(jnp.float32)
            sq = jnp.sum(pf * pf, axis=0, keepdims=True)
            b = y[half:half + kp] + y[full:full + kp]
            rows = lax.broadcasted_iota(jnp.int32, (kp, tile), 0)
            yall[i, 0:half] = y[0:half]
            yall[i, half:half + kp] = jnp.where(rows == kp - 1, sq, b)
            yall[i, half + kp:full] = y[half + kp:full]
            core_copy(i).start()

        @pl.when(i == 0)
        def _():
            s_core_copy().wait_recv()
            sloc[1] = sloc[0] + srecvc[...]
            for d in range(1, chips):
                s_x_copy(d).start()

        @pl.when(i > 0)
        def _():
            j = i - 1
            core_copy(j).wait_recv()
            bh = yall[j, pl.ds(b_rows, kh)] + recvc[j, pl.ds(pl.multiple_of(b_rows - shift, 8), kh)]
            bown[j] = bh
            for d in range(1, chips):
                r = pl.multiple_of(core * (half + kp) + partner(d) * own, 8)
                sendx[d - 1, j, 0:own] = (
                    yall[j, pl.ds(r, own)] + recvc[j, pl.ds(pl.multiple_of(r - shift, 8), own)])
                sendx[d - 1, j, own:own + kh] = bh
                x_copy(j, d).start()
            cols = pl.ds(pl.multiple_of(j * tile, tile), tile)
            cross_ref[:, cols] = (
                yall[j, pl.ds(own_rows, own)]
                + recvc[j, pl.ds(pl.multiple_of(own_rows - shift, 8), own)])

        return carry

    lax.fori_loop(0, tiles + 1, produce, 0)

    total = sloc[1]
    for d in range(1, chips):
        s_x_copy(d).wait_recv()
        total = total + srecvx[d - 1]
    gram = total[:, 2 * half:2 * half + kp] + total[:, 2 * half + kp:2 * half + 2 * kp]
    side = jnp.zeros((kp, 128 - kp), jnp.float32)
    row = lax.broadcasted_iota(jnp.int32, (kp, 128), 0)
    lane = lax.broadcasted_iota(jnp.int32, (kp, 128), 1)
    eye = jnp.where((row == lane) & (row < k), 1.0, 0.0)

    def eliminate(j, carry):
        left, right = carry
        col = jnp.sum(jnp.where(lane == j, left, 0.0), axis=1, keepdims=True)
        pick = row == j
        pivot = jnp.sum(jnp.where(pick[:, 0:1], col, 0.0), axis=0, keepdims=True)
        factor = jnp.where(row[:, 0:1] > j, col, 0.0) / pivot
        lrow = jnp.sum(jnp.where(pick, left, 0.0), axis=0, keepdims=True)
        rrow = jnp.sum(jnp.where(pick, right, 0.0), axis=0, keepdims=True)
        return left - factor * lrow, right - factor * rrow

    left, right = lax.fori_loop(0, k, eliminate, (jnp.concatenate([gram, side], axis=1), eye))
    diag = jnp.sum(jnp.where(row == lane, left, 0.0), axis=1, keepdims=True)
    diag = jnp.where(row[:, 0:1] < k, diag, 1.0)
    inverse = right / jnp.sqrt(diag)

    sgt = jnp.concatenate(
        [total[:, 0:2 * half], jnp.zeros((128 - kp, 2 * half), jnp.float32)], axis=0).T
    ut = lax.dot_general(sgt, inverse, LAST, precision=HI, preferred_element_type=jnp.float32)
    gv = sgt[:, kp - 1:kp] - jnp.sum(ut * ut, axis=1, keepdims=True)
    uts[...] = jnp.concatenate([ut, jnp.zeros((2 * half, 128 - kp), jnp.float32)], axis=1)
    gvs[...] = jnp.broadcast_to(gv, gvs.shape)
    mine = pl.ds(pl.multiple_of(core * half + chip * own, 8), own)

    def collect(i, carry):
        @pl.when(i < tiles)
        def _():
            cols = pl.ds(pl.multiple_of(i * tile, tile), tile)
            for d in range(1, chips):
                x_copy(i, d).wait_recv()
                bown[i] = bown[i] + recvx[d - 1, i, own:own + kh]
                cross_ref[:, cols] = cross_ref[:, cols] + recvx[d - 1, i, 0:own]
            b_copy(i).start()

        @pl.when(i > 0)
        def _():
            j = i - 1
            cols = pl.ds(pl.multiple_of(j * tile, tile), tile)
            b_copy(j).wait_recv()
            btmp[pl.ds(pl.multiple_of(core * kh, 8), kh), :] = bown[j]
            btmp[pl.ds(pl.multiple_of((1 - core) * kh, 8), kh), :] = brecv[j]
            bt = btmp[...]
            v = jnp.dot(inverse[:, 0:kp], bt, precision=HI, preferred_element_type=jnp.float32)
            pv = bt[kp - 1:kp] - jnp.sum(v * v, axis=0, keepdims=True)
            cross = cross_ref[:, cols] - jnp.dot(
                uts[mine, 0:kp], v, precision=HI, preferred_element_type=jnp.float32)
            scale = lax.rsqrt(gvs[mine, 0:1] * pv - cross * cross)
            cross_ref[:, cols] = cross * (dof ** 0.5) * scale

        return carry

    lax.fori_loop(0, tiles + 1, collect, 0)

    def drain(i, carry):
        core_copy(i).wait_send()
        b_copy(i).wait_send()
        for d in range(1, chips):
            x_copy(i, d).wait_send()
        return carry

    lax.fori_loop(0, tiles, drain, 0)
    s_core_copy().wait_send()
    for d in range(1, chips):
        s_x_copy(d).wait_send()


def per_device(dosage, phenotype, covariates):
    rows, snps = dosage.shape
    verts = phenotype.shape[1]
    k = covariates.shape[1] + 1
    parts = lax.axis_size("subj")
    chips = parts // CORES
    own = snps // parts
    half = chips * own
    kp = -(-(k + 1) // 16) * 16
    kh = kp // 2
    tile = next(t for t in (512, 256, 128) if verts % t == 0)
    tiles = verts // tile
    wide = 2 * half + -(-2 * kp // 128) * 128

    f32 = jnp.float32
    vmem = pl.BlockSpec(memory_space=pltpu.VMEM)
    dma = pltpu.SemaphoreType.DMA
    others = chips - 1
    return pl.pallas_call(
        functools.partial(
            exchange_kernel, chips, own, k, kp, tile, float(rows * parts - k - 1)),
        out_shape=jax.ShapeDtypeStruct((own, verts), f32),
        in_specs=[vmem, vmem, pl.BlockSpec(memory_space=pl.ANY)],
        out_specs=vmem,
        scratch_shapes=[
            pltpu.VMEM((2 * half + 2 * kp, rows), jnp.bfloat16),
            pltpu.VMEM((rows, 128), f32),
            pltpu.VMEM((2 * half, 128), f32),
            pltpu.VMEM((2 * half, 128), f32),
            pltpu.VMEM((kp, tile), f32),
            pltpu.VMEM((2, rows, tile), jnp.bfloat16),
            pltpu.VMEM((tiles, 2 * half + kp, tile), f32),
            pltpu.VMEM((tiles, half + kp, tile), f32),
            pltpu.VMEM((others, tiles, own + kh, tile), f32),
            pltpu.VMEM((others, tiles, own + kh, tile), f32),
            pltpu.VMEM((tiles, kh, tile), f32),
            pltpu.VMEM((tiles, kh, tile), f32),
            pltpu.VMEM((2, kp, wide), f32),
            pltpu.VMEM((kp, wide), f32),
            pltpu.VMEM((others, kp, wide), f32),
            dma((2,)),
            dma((tiles,)), dma((tiles,)),
            dma((others, tiles)), dma((others, tiles)),
            dma((tiles,)), dma((tiles,)),
            dma, dma,
            dma((others,)), dma((others,)),
        ],
        compiler_params=pltpu.CompilerParams(
            collective_id=0, has_side_effects=True, vmem_limit_bytes=56 * 1024 * 1024
        ),
        cost_estimate=pl.CostEstimate(
            flops=2 * rows * verts * (2 * half + 2 * kp),
            bytes_accessed=2 * rows * verts + 8 * own * verts, transcendentals=0),
    )(dosage, covariates, phenotype)


def solution(mesh):
    in_specs = (P(("grp", "subj"), None), P(("grp", "subj"), "vert"), P(("grp", "subj"), None))
    out_specs = P(("grp", "subj"), "vert")
    return jax.shard_map(
        per_device, mesh=mesh, in_specs=in_specs, out_specs=out_specs, check_vma=False
    )
```
